32 devices in a mesh: dp: 4 (over y, core), row: 2 (over x), col: 4 (over z).
Axes of the slice: x: 2, y: 2, z: 4, core: 2. Of those that a mesh axis runs over, the one named last changes fastest.
Arguments:
- tokens: bfloat16 [1024, 6144], P(('dp', 'col'), 'row'), may hold values from -6 to 6
- cotangent: bfloat16 [1024, 6144], P(('dp', 'col'), 'row'), may hold values from -6 to 6
- pre_act: bfloat16 [1024, 12288], P('dp', 'col'), may hold values from -6 to 6
- weight_in: bfloat16 [6144, 12288], P('row', 'col'), may hold values from -0.078125 to 0.078125
- weight_out: bfloat16 [12288, 6144], P('col', 'row'), may hold values from -0.0546875 to 0.0546875
Outputs:
- grad_tokens: bfloat16 [1024, 6144], P(('dp', 'col'), 'row')
- grad_in: float32 [6144, 12288], P('row', ('col', 'dp'))
- grad_out: float32 [12288, 6144], P(('col', 'dp'), 'row')
The draws below stay inside these ranges and needn't reach their ends.
All inputs are finite; a program needn't handle non-finite values.
Results may differ from the reference program's by a relative error of at most 0.023.
Values may be sent and summed in bfloat16 or wider, within the bound.
A program may use at most 192 MiB of HBM per device.

```python
import jax
import jax.numpy as jnp
from jax import lax

D = 6144
FF = 12288
TOKC = 64
TOKENS = 1024
N_DP = 4
N_ROW = 2
N_COL = 4


def block_scale(stream_key, extent, split, low, top_value):
    level = 1.0
    for axis_at, shards_of in split:
        steps = jax.random.uniform(jax.random.fold_in(jax.random.fold_in(stream_key, 6), axis_at), (shards_of,), jnp.float32, low / len(split), top_value / len(split))
        level = level * jnp.repeat(jnp.exp(steps), extent[axis_at] // shards_of).reshape((-1,) + (1,) * (len(extent) - 1 - axis_at))
    return level


def noise(key, shape, deviation, limit, cuts=(), kind=jnp.bfloat16):
    level = block_scale(key, shape, cuts, -0.22, 0.18) if cuts else 1.0
    array = jax.random.normal(key, shape, jnp.float32) * deviation * level
    return jnp.minimum(jnp.maximum(array, -limit), limit).astype(kind)


def setup_inputs(seed: int = 0) -> dict:
    arg_keys = jax.random.split(jax.random.key(seed), 6)
    return {
        "tokens": noise(arg_keys[0], (TOKENS, D), 1.0, 6.0, ((0, 16), (1, 2))),
        "cotangent": noise(arg_keys[1], (TOKENS, D), 1.0, 6.0, ((0, 16), (1, 2))),
        "pre_act": noise(arg_keys[2], (TOKENS, FF), 1.5, 6.0, ((0, 4), (1, 4))),
        "weight_in": noise(arg_keys[3], (D, FF), D ** -0.5, 0.078125, ((0, 2), (1, 4))),
        "weight_out": noise(arg_keys[4], (FF, D), FF ** -0.5, 0.0546875, ((0, 4), (1, 2))),
    }


def gelu_value(a):
    return 0.5 * a * (1.0 + lax.erf(a * 0.7071067811865476))


def gelu_slope(a):
    return 0.5 * (1.0 + lax.erf(a * 0.7071067811865476)) + a * jnp.exp(-0.5 * a * a) * 0.3989422804014327


def rounded(value):
    return lax.optimization_barrier(value.astype(jnp.bfloat16)).astype(jnp.float32)


def reference(tokens, cotangent, pre_act, weight_in, weight_out):
    replica = TOKC * N_COL
    width_block = D // N_ROW
    hidden_block = FF // N_COL
    factor = float(TOKENS) ** -0.5
    tok_sets = tokens.reshape(N_DP, replica, D)
    cot_sets = cotangent.reshape(N_DP, replica, D)
    pre_sets = pre_act.reshape(N_DP, replica, FF)
    out_blocks = weight_out.reshape(FF, N_ROW, width_block).transpose(1, 0, 2)
    in_blocks = weight_in.reshape(D, N_COL, hidden_block).transpose(1, 0, 2)
    contract = (((1,), (1,)), ((), ()))
    lead = (((0,), (0,)), ((), ()))

    def one_replica(carry, item):
        tok_rows, cot_rows, pre_rows = item
        cot_blocks = cot_rows.reshape(replica, N_ROW, width_block).transpose(1, 0, 2)

        def add_width(total, pair):
            part = lax.dot_general(pair[0], pair[1], contract, preferred_element_type=jnp.float32)
            return total + rounded(part), None

        grad_hidden, _ = lax.scan(add_width, jnp.zeros((replica, FF), jnp.float32), (cot_blocks, out_blocks))
        pre_float = pre_rows.astype(jnp.float32)
        grad_pre = (grad_hidden * gelu_slope(pre_float)).astype(jnp.bfloat16)
        hidden = gelu_value(pre_float).astype(jnp.bfloat16)
        pre_blocks = grad_pre.reshape(replica, N_COL, hidden_block).transpose(1, 0, 2)

        def add_hidden(total, pair):
            part = lax.dot_general(pair[0], pair[1], contract, preferred_element_type=jnp.float32)
            return total + rounded(part), None

        grad_rows, _ = lax.scan(add_hidden, jnp.zeros((replica, D), jnp.float32), (pre_blocks, in_blocks))
        first = lax.dot_general(tok_rows, grad_pre, lead, preferred_element_type=jnp.float32) * factor
        second = lax.dot_general(hidden, cot_rows, lead, preferred_element_type=jnp.float32) * factor
        return (carry[0] + rounded(first), carry[1] + rounded(second)), grad_rows.astype(jnp.bfloat16)

    start = (jnp.zeros((D, FF), jnp.float32), jnp.zeros((FF, D), jnp.float32))
    (grad_in, grad_out), grad_sets = lax.scan(one_replica, start, (tok_sets, cot_sets, pre_sets))
    return grad_sets.reshape(TOKENS, D), grad_in, grad_out
```

```python
import functools

import jax
import jax.numpy as jnp
from jax import lax
from jax.experimental import pallas as pl
from jax.experimental.pallas import tpu as pltpu
from jax.sharding import PartitionSpec as P

MESH = pl.DeviceIdType.MESH
NT = (((1,), (1,)), ((), ()))
TN = (((0,), (0,)), ((), ()))


def gelu_parts(a):
    half = 0.5 * (1.0 + lax.erf(a * 0.7071067811865476))
    return half * a, half + a * jnp.exp(-0.5 * a * a) * 0.3989422804014327


def tile_of(extent):
    return 256 if extent % 256 == 0 else 128


def body(
    n_dp, n_row, n_col,
    tok, cot, pre, w_in, w_out,
    tok_all, cot_all, gp_all, hid_all, grad_tok,
    win, wout, hid, slope, part, xrecv, gp, acc, cotg, term, rs,
    w_sem, l_sem, cz_s, cz_r, tz_s, tz_r, y_s, y_r, c_s, c_r,
    h_s, h_r, g_s, g_r, x_s, x_r, rs_s, rs_r,
):
    p, r, z = lax.axis_index("dp"), lax.axis_index("row"), lax.axis_index("col")
    n_y = n_dp // 2
    tokc, width = tok.shape
    rows = n_col * tokc
    hidden = pre.shape[1]
    hc = hidden // n_dp
    partner = p + 1 - 2 * lax.rem(p, 2)

    def dp_off(k):
        return lax.rem(p + k, n_dp)

    def remote(src, dst, send, recv, where):
        return pltpu.make_async_remote_copy(
            src_ref=src, dst_ref=dst, send_sem=send, recv_sem=recv,
            device_id=where, device_id_type=MESH,
        )

    wo = pltpu.make_async_copy(w_out, wout, w_sem.at[0])
    wi = pltpu.make_async_copy(w_in, win, w_sem.at[1])
    own = pltpu.make_async_copy(cot, cotg.at[z], l_sem.at[0])
    wo.start()
    own.start()

    barrier = pltpu.get_barrier_semaphore()
    for axis, me, count in (("dp", p, n_dp), ("row", r, n_row), ("col", z, n_col)):
        for k in range(1, count):
            pl.semaphore_signal(
                barrier, inc=1, device_id={axis: lax.rem(me + k, count)}, device_id_type=MESH
            )
    pl.semaphore_wait(barrier, n_dp + n_row + n_col - 3)

    sends = ((cotg, cot_all, cz_s, cz_r), (tok_all.at[p], tok_all, tz_s, tz_r))

    def z_copy(t, d, s, first):
        group, _, ss, rr = sends[t]
        blk = z - s if d == 0 else z + s
        src = (cot, tok)[t] if first else group.at[blk]
        to = z + 1 if d == 0 else z - 1
        return remote(src, group.at[blk], ss.at[d, s], rr.at[d, s + 1], {"col": to})

    def can_send(d, s):
        return (z - s >= 0) & (z + 1 < n_col) if d == 0 else (z + s < n_col) & (z - 1 >= 0)

    def has(d, s):
        return z - s >= 0 if d == 0 else z + s < n_col

    def y_send(t, src, blk):
        for k in range(1, n_y):
            remote(
                src, sends[t][1].at[p, blk], y_s.at[t, k], y_r.at[t, k], {"dp": dp_off(2 * k)}
            ).start()

    def z_start(t):
        for d in (0, 1):
            @pl.when(can_send(d, 0))
            def _():
                z_copy(t, d, 0, True).start()

    def z_step(t, s):
        for d in (0, 1):
            @pl.when(has(d, s))
            def _():
                blk = z - s if d == 0 else z + s
                group = sends[t][0]
                remote(
                    group.at[blk], group.at[blk], sends[t][2].at[d, s], sends[t][3].at[d, s],
                    {"col": lax.rem(z + 1, n_col)},
                ).wait_recv()
                if s < n_col - 1:
                    @pl.when(can_send(d, s))
                    def _():
                        z_copy(t, d, s, False).start()
                y_send(t, group.at[blk], blk)

    def whole(t, at, send, recv, who):
        return remote(
            sends[t][1].at[at], sends[t][1].at[at], send, recv, {"dp": who}
        )

    z_start(0)
    own_tok = pltpu.make_async_copy(tok, tok_all.at[p, z], l_sem.at[1])
    own_tok.start()
    y_send(0, cot, z)
    y_send(1, tok, z)
    wi.start()

    def gelu_chunk(i):
        step = 32
        def one(j, _):
            at = pl.ds(pl.multiple_of(j * step, step), step)
            a = pre[at, i * hc:(i + 1) * hc].astype(jnp.float32)
            value, sl = gelu_parts(a)
            hid[i, at, :] = value.astype(jnp.bfloat16)
            slope[i, at, :] = sl
            return 0
        lax.fori_loop(0, rows // step, one, 0)

    done = 0
    for s in range(1, n_col):
        upto = (n_dp * s + n_col - 2) // (n_col - 1)
        for i in range(done, upto):
            gelu_chunk(i)
        done = upto
        z_step(0, s)
        if s == min(2, n_col - 1):
            own_tok.wait()
            z_start(1)
    for k in range(1, n_dp):
        q = dp_off(k)
        remote(hid.at[q], hid_all.at[p], h_s.at[k], h_r.at[k], {"dp": q}).start()
    own_hid = pltpu.make_async_copy(hid.at[p], hid_all.at[p], l_sem.at[2])
    own_hid.start()

    own.wait()
    own_cot = pltpu.make_async_copy(cotg, cot_all.at[p], l_sem.at[0])
    own_cot.start()
    remote(cotg, cot_all.at[p], c_s.at[0, 0], c_r.at[0, 0], {"dp": partner}).start()
    wo.wait()

    ht = tile_of(hc)
    for i in range(n_dp):
        def ptile(j, _):
            off = pl.multiple_of(j * ht, ht)
            w = wout[pl.ds(i * hc + off, ht), :]
            lhs = cotg[...].reshape(rows, width)
            out = lax.dot_general(lhs, w, NT, preferred_element_type=jnp.float32)
            part[i, :, pl.ds(off, ht)] = out.astype(jnp.bfloat16)
            return 0
        lax.fori_loop(0, hc // ht, ptile, 0)
        for k in range(1, n_row):
            remote(
                part.at[i], xrecv.at[k - 1, i], x_s.at[k - 1, i], x_r.at[k - 1, i],
                {"row": lax.rem(r + k, n_row)},
            ).start()
    wi.wait()

    tok_steps = 1
    wt = tile_of(width)
    for i in range(n_dp):
        for k in range(1, n_row):
            remote(
                part.at[i], xrecv.at[k - 1, i], x_s.at[k - 1, i], x_r.at[k - 1, i],
                {"row": lax.rem(r + k, n_row)},
            ).wait_recv()
        step = 32
        def one(j, _):
            at = pl.ds(pl.multiple_of(j * step, step), step)
            total = part[i, at, :].astype(jnp.float32)
            for k in range(1, n_row):
                total = total + xrecv[k - 1, i, at, :].astype(jnp.float32)
            gp[i, at, :] = (total * slope[i, at, :]).astype(jnp.bfloat16)
            return 0
        lax.fori_loop(0, rows // step, one, 0)

        @pl.when(p == i)
        def _():
            pltpu.make_async_copy(gp.at[i], gp_all.at[p], l_sem.at[3]).start()

        @pl.when(p != i)
        def _():
            k = lax.rem(i - p + n_dp, n_dp)
            remote(gp.at[i], gp_all.at[p], g_s.at[k], g_r.at[k], {"dp": i}).start()

        def wtile(j, _):
            at = pl.ds(pl.multiple_of(j * wt, wt), wt)
            w = win[at, i * hc:(i + 1) * hc]
            out = lax.dot_general(gp[i], w, NT, preferred_element_type=jnp.float32)
            if i > 0:
                out = acc[:, at] + out
            if i < n_dp - 1:
                acc[:, at] = out
            else:
                term[:, :, at] = out.astype(jnp.bfloat16).reshape(n_col, tokc, wt)
            return 0
        lax.fori_loop(0, width // wt, wtile, 0)
        upto = ((n_col - 1) * (i + 1)) // n_dp
        while tok_steps <= upto:
            z_step(1, tok_steps)
            tok_steps += 1

    for k in range(1, n_col):
        to = lax.rem(z + k, n_col)
        remote(term.at[to], rs.at[k], rs_s.at[k], rs_r.at[k], {"col": to}).start()
    remote(tok_all.at[p], tok_all.at[p], c_s.at[1, 0], c_r.at[1, 0], {"dp": partner}).start()

    for t in (0, 1):
        for k in range(1, n_y):
            q = dp_off(n_dp - 2 * k)
            whole(t, q, y_s.at[t, k], y_r.at[t, k], q).wait_recv()
            whole(t, q, c_s.at[t, k], c_r.at[t, k], partner).start()

    for k in range(1, n_col):
        remote(term.at[z], rs.at[k], rs_s.at[k], rs_r.at[k], {"col": lax.rem(z + k, n_col)}).wait_recv()
    total = term[z].astype(jnp.float32)
    for k in range(1, n_col):
        total = total + rs[k].astype(jnp.float32)
    grad_tok[...] = total.astype(jnp.bfloat16)

    own_hid.wait()
    own_cot.wait()
    pltpu.make_async_copy(gp.at[p], gp_all.at[p], l_sem.at[3]).wait()
    for t in (0, 1):
        for d in (0, 1):
            for s in range(n_col - 1):
                @pl.when(can_send(d, s))
                def _():
                    z_copy(t, d, s, s == 0).wait_send()
        for k in range(1, n_y):
            whole(t, p, y_s.at[t, k], y_r.at[t, k], dp_off(2 * k)).wait_send()
        for k in range(n_y):
            q = dp_off(n_dp - 2 * k) if k else p
            whole(t, q, c_s.at[t, k], c_r.at[t, k], partner).wait()
    for k in range(1, n_dp):
        q = dp_off(k)
        remote(hid.at[q], hid_all.at[p], h_s.at[k], h_r.at[k], {"dp": q}).wait()
        remote(gp.at[q], gp_all.at[p], g_s.at[k], g_r.at[k], {"dp": q}).wait()
    for i in range(n_dp):
        for k in range(1, n_row):
            remote(
                part.at[i], xrecv.at[k - 1, i], x_s.at[k - 1, i], x_r.at[k - 1, i],
                {"row": lax.rem(r + k, n_row)},
            ).wait_send()
    for k in range(1, n_col):
        to = lax.rem(z + k, n_col)
        remote(term.at[to], rs.at[k], rs_s.at[k], rs_r.at[k], {"col": to}).wait_send()


def shards(n_dp, n_row, n_col, tokens, cotangent, pre_act, weight_in, weight_out):
    tokc, width = tokens.shape
    rows, hidden = pre_act.shape
    hc = hidden // n_dp
    n_y = n_dp // 2
    bf, f32 = jnp.bfloat16, jnp.float32
    dma = pltpu.SemaphoreType.DMA
    anywhere = pl.BlockSpec(memory_space=pl.ANY)
    vmem = pl.BlockSpec(memory_space=pltpu.VMEM)
    tok_all, cot_all, gp_all, hid_all, grad_tokens = pl.pallas_call(
        functools.partial(body, n_dp, n_row, n_col),
        out_shape=(
            jax.ShapeDtypeStruct((n_dp, n_col, tokc, width), bf),
            jax.ShapeDtypeStruct((n_dp, n_col, tokc, width), bf),
            jax.ShapeDtypeStruct((n_dp, rows, hc), bf),
            jax.ShapeDtypeStruct((n_dp, rows, hc), bf),
            jax.ShapeDtypeStruct((tokc, width), bf),
        ),
        in_specs=[anywhere, anywhere, vmem, anywhere, anywhere],
        out_specs=(anywhere, anywhere, anywhere, anywhere, vmem),
        scratch_shapes=[
            pltpu.VMEM((width, hidden), bf),
            pltpu.VMEM((hidden, width), bf),
            pltpu.VMEM((n_dp, rows, hc), bf),
            pltpu.VMEM((n_dp, rows, hc), f32),
            pltpu.VMEM((n_dp, rows, hc), bf),
            pltpu.VMEM((max(n_row - 1, 1), n_dp, rows, hc), bf),
            pltpu.VMEM((n_dp, rows, hc), bf),
            pltpu.VMEM((rows, width), f32),
            pltpu.VMEM((n_col, tokc, width), bf),
            pltpu.VMEM((n_col, tokc, width), bf),
            pltpu.VMEM((n_col, tokc, width), bf),
            dma((2,)), dma((4,)),
            dma((2, n_col)), dma((2, n_col)), dma((2, n_col)), dma((2, n_col)),
            dma((2, n_y)), dma((2, n_y)), dma((2, n_y)), dma((2, n_y)),
            dma((n_dp,)), dma((n_dp,)), dma((n_dp,)), dma((n_dp,)),
            dma((max(n_row - 1, 1), n_dp)), dma((max(n_row - 1, 1), n_dp)),
            dma((n_col,)), dma((n_col,)),
        ],
        compiler_params=pltpu.CompilerParams(
            collective_id=0, has_side_effects=True, vmem_limit_bytes=62 * 1024 * 1024
        ),
    )(tokens, cotangent, pre_act, weight_in, weight_out)
    total = n_dp * rows
    factor = float(total) ** (-0.5)
    tok_all, cot_all = tok_all.reshape(total, width), cot_all.reshape(total, width)
    gp_all, hid_all = gp_all.reshape(total, hc), hid_all.reshape(total, hc)
    grad_in = lax.dot_general(tok_all, gp_all, TN, preferred_element_type=f32) * factor
    grad_out = lax.dot_general(hid_all, cot_all, TN, preferred_element_type=f32) * factor
    return grad_tokens, grad_in, grad_out


def solution(mesh):
    in_specs = (
        P(("dp", "col"), "row"),
        P(("dp", "col"), "row"),
        P("dp", "col"),
        P("row", "col"),
        P("col", "row"),
    )
    out_specs = (P(("dp", "col"), "row"), P("row", ("col", "dp")), P(("col", "dp"), "row"))
    sizes = (mesh.shape["dp"], mesh.shape["row"], mesh.shape["col"])
    return jax.shard_map(
        functools.partial(shards, *sizes),
        mesh=mesh, in_specs=in_specs, out_specs=out_specs, check_vma=False,
    )
```

```python
import functools

import jax
import jax.numpy as jnp
from jax import lax
from jax.experimental import pallas as pl
from jax.experimental.pallas import tpu as pltpu
from jax.sharding import PartitionSpec as P

MESH = pl.DeviceIdType.MESH
NT = (((1,), (1,)), ((), ()))
TN = (((0,), (0,)), ((), ()))


def gelu_parts(a):
    half = 0.5 * (1.0 + lax.erf(a * 0.7071067811865476))
    return half * a, half + a * jnp.exp(-0.5 * a * a) * 0.3989422804014327


def tile_of(extent):
    return 256 if extent % 256 == 0 else 128


def body(
    n_dp, n_row, n_col,
    tok, cot, pre, w_in, w_out,
    tok_all, cot_all, gp_all, hid_all, grad_tok,
    win, wout, hid, slope, part, xrecv, gp, acc, cotg, term, rs,
    w_sem, l_sem, cz_s, cz_r, tz_s, tz_r, y_s, y_r, c_s, c_r,
    h_s, h_r, hf_s, hf_r, g_s, g_r, gf_s, gf_r, x_s, x_r, rs_s, rs_r,
):
    p, r, z = lax.axis_index("dp"), lax.axis_index("row"), lax.axis_index("col")
    n_y = n_dp // 2
    _, half_c, width = tok.shape
    half = n_col * half_c
    piece = half // n_row
    hidden = pre.shape[1]
    hc = hidden // n_dp
    y, c = p // 2, lax.rem(p, 2)
    partner = 2 * y + 1 - c

    def peer(m, sign=1):
        there = lax.rem(y + sign * (m // 2) + n_y, n_y)
        return 2 * there + (1 - c if m % 2 else c)

    def remote(src, dst, send, recv, where):
        return pltpu.make_async_remote_copy(
            src_ref=src, dst_ref=dst, send_sem=send, recv_sem=recv,
            device_id=where, device_id_type=MESH,
        )

    wo = pltpu.make_async_copy(w_out, wout, w_sem.at[0])
    wi = pltpu.make_async_copy(w_in, win, w_sem.at[1])
    own = pltpu.make_async_copy(cot, cotg.at[:, z], l_sem.at[0])
    wo.start()
    own.start()

    barrier = pltpu.get_barrier_semaphore()
    for axis, me, count in (("dp", p, n_dp), ("row", r, n_row), ("col", z, n_col)):
        for k in range(1, count):
            pl.semaphore_signal(
                barrier, inc=1, device_id={axis: lax.rem(me + k, count)}, device_id_type=MESH
            )
    pl.semaphore_wait(barrier, n_dp + n_row + n_col - 3)

    def block(t, blk):
        return cotg.at[t, blk] if t < 2 else tok_all.at[p, :, blk]

    def landing(t, blk):
        return cot_all.at[p, t, blk] if t < 2 else tok_all.at[p, :, blk]

    def full(t, q):
        return cot_all.at[q, t] if t < 2 else tok_all.at[q]

    def sems(t):
        return (cz_s.at[t], cz_r.at[t]) if t < 2 else (tz_s.at[0], tz_r.at[0])

    def z_copy(t, d, s):
        blk = z - s if d == 0 else z + s
        src = block(t, blk) if s else (cot.at[t] if t < 2 else tok)
        ss, rr = sems(t)
        to = z + 1 if d == 0 else z - 1
        return remote(src, block(t, blk), ss.at[d, s], rr.at[d, s + 1], {"col": to})

    def has(d, s):
        return z - s >= 0 if d == 0 else z + s < n_col

    def can_send(d, s):
        return has(d, s) & (z + 1 < n_col if d == 0 else z - 1 >= 0)

    def y_send(t, src, blk):
        for k in range(1, n_y):
            remote(
                src, landing(t, blk), y_s.at[t, k], y_r.at[t, k], {"dp": peer(2 * k)}
            ).start()

    def z_start(t):
        for d in (0, 1):
            @pl.when(can_send(d, 0))
            def _():
                z_copy(t, d, 0).start()

    def z_step(t, s):
        ss, rr = sems(t)
        for d in (0, 1):
            @pl.when(has(d, s))
            def _():
                blk = z - s if d == 0 else z + s
                remote(
                    block(t, blk), block(t, blk), ss.at[d, s], rr.at[d, s],
                    {"col": lax.rem(z + 1, n_col)},
                ).wait_recv()
                if s < n_col - 1:
                    @pl.when(can_send(d, s))
                    def _():
                        z_copy(t, d, s).start()
                y_send(t, block(t, blk), blk)

    def whole(t, at, send, recv, who):
        return remote(full(t, at), full(t, at), send, recv, {"dp": who})

    z_start(0)
    own_tok = pltpu.make_async_copy(tok, tok_all.at[p, :, z], l_sem.at[1])
    own_tok.start()
    y_send(0, cot.at[0], z)
    y_send(1, cot.at[1], z)
    y_send(2, tok, z)
    wi.start()

    def gelu_chunk(i):
        def one(j, _):
            at = pl.ds(pl.multiple_of(j * half_c, half_c), half_c)
            to = pl.ds(pl.multiple_of((j // 2) * half_c, half_c), half_c)
            a = pre[at, i * hc:(i + 1) * hc].astype(jnp.float32)
            value, sl = gelu_parts(a)
            hid[i, lax.rem(j, 2), to, :] = value.astype(jnp.bfloat16)
            slope[i, lax.rem(j, 2), to, :] = sl
            return 0
        lax.fori_loop(0, 2 * n_col, one, 0)

    done = 0
    for s in range(1, n_col):
        upto = (n_dp * s + n_col - 2) // (n_col - 1)
        for i in range(done, upto):
            gelu_chunk(i)
        done = upto
        z_step(0, s)
        if s == 1:
            z_start(1)

    rows_of = pl.ds(pl.multiple_of(r * piece, piece), piece)

    def hid_copy(m):
        q = peer(m)
        if m == 1:
            src, dst = hid.at[q], hid_all.at[p]
        else:
            src, dst = hid.at[q, :, rows_of], hid_all.at[p, :, rows_of]
        return remote(src, dst, h_s.at[m], h_r.at[m], {"dp": q})

    def hid_pass(m, k):
        ref = hid_all.at[peer(m, -1), :, rows_of]
        return remote(ref, ref, hf_s.at[m, k], hf_r.at[m, k], {"row": lax.rem(r + k, n_row)})

    def gp_copy(h, m):
        q = peer(m)
        if m == 1:
            src, dst = gp.at[q, h], gp_all.at[p, h]
        else:
            src, dst = gp.at[q, h, rows_of], gp_all.at[p, h, rows_of]
        return remote(src, dst, g_s.at[h, m], g_r.at[h, m], {"dp": q})

    def gp_pass(h, m, k):
        ref = gp_all.at[peer(m, -1), h, rows_of]
        return remote(
            ref, ref, gf_s.at[h, m, k], gf_r.at[h, m, k], {"row": lax.rem(r + k, n_row)}
        )

    for m in range(1, n_dp):
        hid_copy(m).start()
    own_hid = pltpu.make_async_copy(hid.at[p], hid_all.at[p], l_sem.at[2])
    own_hid.start()

    own.wait()
    wo.wait()
    ht = tile_of(hc)
    order = list(range(2, n_dp)) + [0, 1]

    def x_copy(h, m, k):
        q = peer(m)
        return remote(
            part.at[q, h], xrecv.at[k - 1, q, h], x_s.at[k - 1, h, m], x_r.at[k - 1, h, m],
            {"row": lax.rem(r + k, n_row)},
        )

    def part_chunk(h, m):
        q = peer(m)
        def ptile(j, _):
            off = pl.multiple_of(j * ht, ht)
            w = wout[pl.ds(pl.multiple_of(q * hc + off, ht), ht), :]
            lhs = cotg[h].reshape(half, width)
            out = lax.dot_general(lhs, w, NT, preferred_element_type=jnp.float32)
            part[q, h, :, pl.ds(off, ht)] = out.astype(jnp.bfloat16)
            return 0
        lax.fori_loop(0, hc // ht, ptile, 0)
        for k in range(1, n_row):
            x_copy(h, m, k).start()

    b_steps = 1
    for at, m in enumerate(order):
        part_chunk(0, m)
        upto = -(-(n_col - 1) * (at + 1) // n_dp)
        while b_steps <= upto:
            z_step(1, b_steps)
            if b_steps == min(2, n_col - 1):
                own_tok.wait()
                z_start(2)
            b_steps += 1
    for m in order:
        part_chunk(1, m)

    own_cot = pltpu.make_async_copy(cotg, cot_all.at[p], l_sem.at[0])
    own_cot.start()
    for t in (0, 1):
        remote(cotg.at[t], cot_all.at[p, t], c_s.at[t, 0], c_r.at[t, 0], {"dp": partner}).start()
    wi.wait()

    wt = tile_of(width)
    tok_steps = 1
    for h in (0, 1):
        for at, m in enumerate(order):
            q = peer(m)
            for k in range(1, n_row):
                x_copy(h, m, k).wait_recv()
            def one(j, _):
                rows = pl.ds(pl.multiple_of(j * half_c, half_c), half_c)
                total = part[q, h, rows, :].astype(jnp.float32)
                for k in range(1, n_row):
                    total = total + xrecv[k - 1, q, h, rows, :].astype(jnp.float32)
                gp[q, h, rows, :] = (total * slope[q, h, rows, :]).astype(jnp.bfloat16)
                return 0
            lax.fori_loop(0, n_col, one, 0)
            if m:
                gp_copy(h, m).start()
            else:
                pltpu.make_async_copy(gp.at[p, h], gp_all.at[p, h], l_sem.at[3]).start()

            def wtile(j, _):
                cols = pl.ds(pl.multiple_of(j * wt, wt), wt)
                w = win[cols, pl.ds(pl.multiple_of(q * hc, hc), hc)]
                out = lax.dot_general(gp[q, h], w, NT, preferred_element_type=jnp.float32)
                if at > 0:
                    out = acc[:, cols] + out
                if at < n_dp - 1:
                    acc[:, cols] = out
                else:
                    term[h, :, :, cols] = out.astype(jnp.bfloat16).reshape(n_col, half_c, wt)
                return 0
            lax.fori_loop(0, width // wt, wtile, 0)
            upto = -(-(n_col - 1) * (at + 1 + h * n_dp) // (n_dp + n_dp // 2))
            while tok_steps <= min(upto, n_col - 1):
                z_step(2, tok_steps)
                tok_steps += 1
        for k in range(1, n_col):
            rs_copy(remote, term, rs, rs_s, rs_r, h, k, z, n_col).start()
        if h == 0:
            for m in range(2, n_dp):
                hid_copy(m).wait_recv()
                for k in range(1, n_row):
                    hid_pass(m, k).start()
            for t in (0, 1):
                for k in range(1, n_y):
                    q = peer(2 * k, -1)
                    whole(t, q, y_s.at[t, k], y_r.at[t, k], q).wait_recv()
                    whole(t, q, c_s.at[t, k], c_r.at[t, k], partner).start()
    whole(2, p, c_s.at[2, 0], c_r.at[2, 0], partner).start()

    for h in (0, 1):
        for m in range(2, n_dp):
            gp_copy(h, m).wait_recv()
            for k in range(1, n_row):
                gp_pass(h, m, k).start()
    for k in range(1, n_y):
        q = peer(2 * k, -1)
        whole(2, q, y_s.at[2, k], y_r.at[2, k], q).wait_recv()
        whole(2, q, c_s.at[2, k], c_r.at[2, k], partner).start()

    for h in (0, 1):
        for k in range(1, n_col):
            rs_copy(remote, term, rs, rs_s, rs_r, h, k, z, n_col).wait_recv()
        total = term[h, z].astype(jnp.float32)
        for k in range(1, n_col):
            total = total + rs[h, k].astype(jnp.float32)
        grad_tok[h] = total.astype(jnp.bfloat16)

    own_hid.wait()
    own_cot.wait()
    pltpu.make_async_copy(gp.at[p], gp_all.at[p], l_sem.at[3]).wait()
    for t in (0, 1, 2):
        for d in (0, 1):
            for s in range(n_col - 1):
                @pl.when(can_send(d, s))
                def _():
                    z_copy(t, d, s).wait_send()
        for k in range(1, n_y):
            whole(t, p, y_s.at[t, k], y_r.at[t, k], peer(2 * k)).wait_send()
        for k in range(n_y):
            q = peer(2 * k, -1)
            whole(t, q, c_s.at[t, k], c_r.at[t, k], partner).wait()
    for m in range(1, n_dp):
        hid_copy(m).wait_send()
        if m == 1:
            hid_copy(m).wait_recv()
        else:
            for k in range(1, n_row):
                hid_pass(m, k).wait()
        for h in (0, 1):
            gp_copy(h, m).wait_send()
            if m == 1:
                gp_copy(h, m).wait_recv()
            else:
                for k in range(1, n_row):
                    gp_pass(h, m, k).wait()
    for h in (0, 1):
        for m in range(n_dp):
            for k in range(1, n_row):
                x_copy(h, m, k).wait_send()
        for k in range(1, n_col):
            rs_copy(remote, term, rs, rs_s, rs_r, h, k, z, n_col).wait_send()


def rs_copy(remote, term, rs, rs_s, rs_r, h, k, z, n_col):
    to = lax.rem(z + k, n_col)
    return remote(term.at[h, to], rs.at[h, k], rs_s.at[h, k], rs_r.at[h, k], {"col": to})


def shards(n_dp, n_row, n_col, tokens, cotangent, pre_act, weight_in, weight_out):
    tokc, width = tokens.shape
    rows, hidden = pre_act.shape
    hc = hidden // n_dp
    n_y = n_dp // 2
    bf, f32 = jnp.bfloat16, jnp.float32
    dma = pltpu.SemaphoreType.DMA
    anywhere = pl.BlockSpec(memory_space=pl.ANY)
    vmem = pl.BlockSpec(memory_space=pltpu.VMEM)
    half_c, half, xs = tokc // 2, rows // 2, max(n_row - 1, 1)
    tok_all, cot_all, gp_all, hid_all, grad_tokens = pl.pallas_call(
        functools.partial(body, n_dp, n_row, n_col),
        out_shape=(
            jax.ShapeDtypeStruct((n_dp, 2, n_col, half_c, width), bf),
            jax.ShapeDtypeStruct((n_dp, 2, n_col, half_c, width), bf),
            jax.ShapeDtypeStruct((n_dp, 2, half, hc), bf),
            jax.ShapeDtypeStruct((n_dp, 2, half, hc), bf),
            jax.ShapeDtypeStruct((2, half_c, width), bf),
        ),
        in_specs=[anywhere, anywhere, vmem, anywhere, anywhere],
        out_specs=(anywhere, anywhere, anywhere, anywhere, vmem),
        scratch_shapes=[
            pltpu.VMEM((width, hidden), bf),
            pltpu.VMEM((hidden, width), bf),
            pltpu.VMEM((n_dp, 2, half, hc), bf),
            pltpu.VMEM((n_dp, 2, half, hc), f32),
            pltpu.VMEM((n_dp, 2, half, hc), bf),
            pltpu.VMEM((xs, n_dp, 2, half, hc), bf),
            pltpu.VMEM((n_dp, 2, half, hc), bf),
            pltpu.VMEM((half, width), f32),
            pltpu.VMEM((2, n_col, half_c, width), bf),
            pltpu.VMEM((2, n_col, half_c, width), bf),
            pltpu.VMEM((2, n_col, half_c, width), bf),
            dma((2,)), dma((4,)),
            dma((2, 2, n_col)), dma((2, 2, n_col)), dma((1, 2, n_col)), dma((1, 2, n_col)),
            dma((3, n_y)), dma((3, n_y)), dma((3, n_y)), dma((3, n_y)),
            dma((n_dp,)), dma((n_dp,)), dma((n_dp, n_row)), dma((n_dp, n_row)),
            dma((2, n_dp)), dma((2, n_dp)), dma((2, n_dp, n_row)), dma((2, n_dp, n_row)),
            dma((xs, 2, n_dp)), dma((xs, 2, n_dp)),
            dma((2, n_col)), dma((2, n_col)),
        ],
        compiler_params=pltpu.CompilerParams(
            collective_id=0, has_side_effects=True, vmem_limit_bytes=62 * 1024 * 1024
        ),
    )(
        tokens.reshape(2, half_c, width), cotangent.reshape(2, half_c, width),
        pre_act, weight_in, weight_out,
    )
    grad_tokens = grad_tokens.reshape(tokc, width)
    total = n_dp * rows
    factor = float(total) ** (-0.5)
    tok_all, cot_all = tok_all.reshape(total, width), cot_all.reshape(total, width)
    gp_all, hid_all = gp_all.reshape(total, hc), hid_all.reshape(total, hc)
    grad_in = lax.dot_general(tok_all, gp_all, TN, preferred_element_type=f32) * factor
    grad_out = lax.dot_general(hid_all, cot_all, TN, preferred_element_type=f32) * factor
    return grad_tokens, grad_in, grad_out


def solution(mesh):
    in_specs = (
        P(("dp", "col"), "row"),
        P(("dp", "col"), "row"),
        P("dp", "col"),
        P("row", "col"),
        P("col", "row"),
    )
    out_specs = (P(("dp", "col"), "row"), P("row", ("col", "dp")), P(("col", "dp"), "row"))
    sizes = (mesh.shape["dp"], mesh.shape["row"], mesh.shape["col"])
    return jax.shard_map(
        functools.partial(shards, *sizes),
        mesh=mesh, in_specs=in_specs, out_specs=out_specs, check_vma=False,
    )
```

```python
import functools

import jax
import jax.numpy as jnp
from jax import lax
from jax.experimental import pallas as pl
from jax.experimental.pallas import tpu as pltpu
from jax.sharding import PartitionSpec as P

MESH = pl.DeviceIdType.MESH
NT = (((1,), (1,)), ((), ()))
TN = (((0,), (0,)), ((), ()))


def gelu_parts(a):
    half = 0.5 * (1.0 + lax.erf(a * 0.7071067811865476))
    return half * a, half + a * jnp.exp(-0.5 * a * a) * 0.3989422804014327


def tile_of(extent):
    return 256 if extent % 256 == 0 else 128


def body(
    n_dp, n_row, n_col, factor,
    tok, cot, pre, w_in, w_out,
    tok_all, cot_all, gp_all, hid_all, grad_tok, rounded,
    win, wout, hid, slope, part, xrecv, gp, acc, cotg, term, rs, flipped,
    w_sem, l_sem, cz_s, cz_r, tz_s, tz_r, y_s, y_r, c_s, c_r,
    h_s, h_r, hf_s, hf_r, g_s, g_r, gf_s, gf_r, x_s, x_r, rs_s, rs_r,
):
    p, r, z = lax.axis_index("dp"), lax.axis_index("row"), lax.axis_index("col")
    n_y = n_dp // 2
    _, half_c, width = tok.shape
    half = n_col * half_c
    piece = half // n_row
    hidden = pre.shape[1]
    hc = hidden // n_dp
    y, c = p // 2, lax.rem(p, 2)
    partner = 2 * y + 1 - c

    def peer(m, sign=1):
        there = lax.rem(y + sign * (m // 2) + n_y, n_y)
        return 2 * there + (1 - c if m % 2 else c)

    def remote(src, dst, send, recv, where):
        return pltpu.make_async_remote_copy(
            src_ref=src, dst_ref=dst, send_sem=send, recv_sem=recv,
            device_id=where, device_id_type=MESH,
        )

    wo = pltpu.make_async_copy(w_out, wout.at[pl.ds(0, hidden)], w_sem.at[0])
    wi = pltpu.make_async_copy(w_in, win, w_sem.at[1])
    own = pltpu.make_async_copy(cot, cotg.at[:, z], l_sem.at[0])
    wo.start()
    own.start()

    barrier = pltpu.get_barrier_semaphore()
    for axis, me, count in (("dp", p, n_dp), ("row", r, n_row), ("col", z, n_col)):
        for k in range(1, count):
            pl.semaphore_signal(
                barrier, inc=1, device_id={axis: lax.rem(me + k, count)}, device_id_type=MESH
            )
    pl.semaphore_wait(barrier, n_dp + n_row + n_col - 3)

    def block(t, blk):
        return cotg.at[t, blk] if t < 2 else tok_all.at[p, :, blk]

    def landing(t, blk):
        return cot_all.at[p, t, blk] if t < 2 else tok_all.at[p, :, blk]

    def full(t, q):
        return cot_all.at[q, t] if t < 2 else tok_all.at[q]

    def sems(t):
        return (cz_s.at[t], cz_r.at[t]) if t < 2 else (tz_s.at[0], tz_r.at[0])

    def z_copy(t, d, s):
        blk = z - s if d == 0 else z + s
        src = block(t, blk) if s else (cot.at[t] if t < 2 else tok)
        ss, rr = sems(t)
        to = z + 1 if d == 0 else z - 1
        return remote(src, block(t, blk), ss.at[d, s], rr.at[d, s + 1], {"col": to})

    def has(d, s):
        return z - s >= 0 if d == 0 else z + s < n_col

    def can_send(d, s):
        return has(d, s) & (z + 1 < n_col if d == 0 else z - 1 >= 0)

    def y_send(t, src, blk):
        for k in range(1, n_y):
            remote(
                src, landing(t, blk), y_s.at[t, k], y_r.at[t, k], {"dp": peer(2 * k)}
            ).start()

    def z_start(t):
        for d in (0, 1):
            @pl.when(can_send(d, 0))
            def _():
                z_copy(t, d, 0).start()

    def z_step(t, s):
        ss, rr = sems(t)
        for d in (0, 1):
            @pl.when(has(d, s))
            def _():
                blk = z - s if d == 0 else z + s
                remote(
                    block(t, blk), block(t, blk), ss.at[d, s], rr.at[d, s],
                    {"col": lax.rem(z + 1, n_col)},
                ).wait_recv()
                if s < n_col - 1:
                    @pl.when(can_send(d, s))
                    def _():
                        z_copy(t, d, s).start()
                y_send(t, block(t, blk), blk)

    def whole(t, at, send, recv, who):
        return remote(full(t, at), full(t, at), send, recv, {"dp": who})

    z_start(0)
    own_tok = pltpu.make_async_copy(tok, tok_all.at[p, :, z], l_sem.at[1])
    own_tok.start()
    y_send(0, cot.at[0], z)
    y_send(1, cot.at[1], z)
    y_send(2, tok, z)
    wi.start()

    def gelu_chunk(i):
        def one(j, _):
            at = pl.ds(pl.multiple_of(j * half_c, half_c), half_c)
            to = pl.ds(pl.multiple_of((j // 2) * half_c, half_c), half_c)
            a = pre[at, i * hc:(i + 1) * hc].astype(jnp.float32)
            value, sl = gelu_parts(a)
            hid[i, lax.rem(j, 2), to, :] = value.astype(jnp.bfloat16)
            slope[i, lax.rem(j, 2), to, :] = sl
            return 0
        lax.fori_loop(0, 2 * n_col, one, 0)

    done = 0
    for s in range(1, n_col):
        upto = (n_dp * s + n_col - 2) // (n_col - 1)
        for i in range(done, upto):
            gelu_chunk(i)
        done = upto
        z_step(0, s)
        if s == 1:
            z_start(1)

    rows_of = pl.ds(pl.multiple_of(r * piece, piece), piece)

    def hid_copy(m):
        q = peer(m)
        if m == 1:
            src, dst = hid.at[q], hid_all.at[p]
        else:
            src, dst = hid.at[q, :, rows_of], hid_all.at[p, :, rows_of]
        return remote(src, dst, h_s.at[m], h_r.at[m], {"dp": q})

    def hid_pass(m, k):
        ref = hid_all.at[peer(m, -1), :, rows_of]
        return remote(ref, ref, hf_s.at[m, k], hf_r.at[m, k], {"row": lax.rem(r + k, n_row)})

    def gp_copy(h, m):
        q = peer(m)
        if m == 1:
            src, dst = gp.at[q, h], gp_all.at[p, h]
        else:
            src, dst = gp.at[q, h, rows_of], gp_all.at[p, h, rows_of]
        return remote(src, dst, g_s.at[h, m], g_r.at[h, m], {"dp": q})

    def gp_pass(h, m, k):
        ref = gp_all.at[peer(m, -1), h, rows_of]
        return remote(
            ref, ref, gf_s.at[h, m, k], gf_r.at[h, m, k], {"row": lax.rem(r + k, n_row)}
        )

    for m in range(1, n_dp):
        hid_copy(m).start()
    own_hid = pltpu.make_async_copy(hid.at[p], hid_all.at[p], l_sem.at[2])
    own_hid.start()

    own.wait()
    wo.wait()
    ht = tile_of(hc)
    order = list(range(2, n_dp)) + [0, 1]

    def x_copy(h, m, k):
        q = peer(m)
        return remote(
            part.at[q, h], xrecv.at[k - 1, q, h], x_s.at[k - 1, h, m], x_r.at[k - 1, h, m],
            {"row": lax.rem(r + k, n_row)},
        )

    def part_chunk(h, m):
        q = peer(m)
        def ptile(j, _):
            off = pl.multiple_of(j * ht, ht)
            w = wout[pl.ds(pl.multiple_of(q * hc + off, ht), ht), :]
            lhs = cotg[h].reshape(half, width)
            out = lax.dot_general(lhs, w, NT, preferred_element_type=jnp.float32)
            part[q, h, :, pl.ds(off, ht)] = out.astype(jnp.bfloat16)
            return 0
        lax.fori_loop(0, hc // ht, ptile, 0)
        for k in range(1, n_row):
            x_copy(h, m, k).start()

    b_steps = 1
    for at, m in enumerate(order):
        part_chunk(0, m)
        upto = -(-(n_col - 1) * (at + 1) // n_dp)
        while b_steps <= upto:
            z_step(1, b_steps)
            if b_steps == min(2, n_col - 1):
                own_tok.wait()
                z_start(2)
            b_steps += 1
    for m in order:
        part_chunk(1, m)

    own_cot = pltpu.make_async_copy(cotg, cot_all.at[p], l_sem.at[0])
    own_cot.start()
    for t in (0, 1):
        remote(cotg.at[t], cot_all.at[p, t], c_s.at[t, 0], c_r.at[t, 0], {"dp": partner}).start()
    wi.wait()

    wt = tile_of(width)
    tok_steps = 1
    for h in (0, 1):
        for at, m in enumerate(order):
            q = peer(m)
            for k in range(1, n_row):
                x_copy(h, m, k).wait_recv()
            def one(j, _):
                rows = pl.ds(pl.multiple_of(j * half_c, half_c), half_c)
                total = part[q, h, rows, :].astype(jnp.float32)
                for k in range(1, n_row):
                    total = total + xrecv[k - 1, q, h, rows, :].astype(jnp.float32)
                gp[q, h, rows, :] = (total * slope[q, h, rows, :]).astype(jnp.bfloat16)
                return 0
            lax.fori_loop(0, n_col, one, 0)
            if m:
                gp_copy(h, m).start()
            else:
                pltpu.make_async_copy(gp.at[p, h], gp_all.at[p, h], l_sem.at[3]).start()

            def wtile(j, _):
                cols = pl.ds(pl.multiple_of(j * wt, wt), wt)
                w = win[cols, pl.ds(pl.multiple_of(q * hc, hc), hc)]
                out = lax.dot_general(gp[q, h], w, NT, preferred_element_type=jnp.float32)
                if at > 0:
                    out = acc[:, cols] + out
                if at < n_dp - 1:
                    acc[:, cols] = out
                else:
                    term[h, :, :, cols] = out.astype(jnp.bfloat16).reshape(n_col, half_c, wt)
                return 0
            lax.fori_loop(0, width // wt, wtile, 0)
            upto = -(-(n_col - 1) * (at + 1 + h * n_dp) // (n_dp + n_dp // 2))
            while tok_steps <= min(upto, n_col - 1):
                z_step(2, tok_steps)
                tok_steps += 1
        for k in range(1, n_col):
            rs_copy(remote, term, rs, rs_s, rs_r, h, k, z, n_col).start()
        if h == 0:
            for m in range(2, n_dp):
                hid_copy(m).wait_recv()
                for k in range(1, n_row):
                    hid_pass(m, k).start()
            for t in (0, 1):
                for k in range(1, n_y):
                    q = peer(2 * k, -1)
                    whole(t, q, y_s.at[t, k], y_r.at[t, k], q).wait_recv()
                    whole(t, q, c_s.at[t, k], c_r.at[t, k], partner).start()
    whole(2, p, c_s.at[2, 0], c_r.at[2, 0], partner).start()

    rows, total = 2 * half, n_dp * 2 * half
    hid_copy(1).wait_recv()
    for m in range(1, n_dp):
        hid_copy(m).wait_send()
        if m > 1:
            for k in range(1, n_row):
                hid_pass(m, k).wait_recv()
    own_hid.wait()
    hid_in = pltpu.make_async_copy(hid_all, hid, l_sem.at[4])
    hid_in.start()
    own_cot.wait()
    for t in (0, 1):
        for k in range(n_y):
            q = peer(2 * k, -1) if k else p
            whole(t, q, c_s.at[t, k], c_r.at[t, k], partner).wait_recv()
    def bring(j, _):
        to = pl.ds(pl.multiple_of(j * half_c, half_c), half_c)
        src = cot_all.at[j // (2 * n_col), lax.rem(j // n_col, 2), lax.rem(j, n_col)]
        pltpu.make_async_copy(src, wout.at[to], l_sem.at[5]).start()
        return 0
    lax.fori_loop(0, n_dp * 2 * n_col, bring, 0)
    hid_in.wait()
    for q in range(n_dp):
        flipped[:, q * rows:(q + 1) * rows] = hid[q].reshape(rows, hc).T
    pltpu.make_async_copy(
        wout.at[pl.ds(0, total)], wout.at[pl.ds(0, total)], l_sem.at[5]
    ).wait()
    def otile(j, _):
        cols = pl.ds(pl.multiple_of(j * wt, wt), wt)
        out = jnp.dot(flipped[...], wout[0:total, cols], preferred_element_type=jnp.float32)
        wout[total:total + hc, cols] = (out * factor).astype(jnp.bfloat16)
        return 0
    lax.fori_loop(0, width // wt, otile, 0)
    out_copy = pltpu.make_async_copy(wout.at[pl.ds(total, hc)], rounded, l_sem.at[6])
    out_copy.start()

    for h in (0, 1):
        for m in range(2, n_dp):
            gp_copy(h, m).wait_recv()
            for k in range(1, n_row):
                gp_pass(h, m, k).start()
    for k in range(1, n_y):
        q = peer(2 * k, -1)
        whole(2, q, y_s.at[2, k], y_r.at[2, k], q).wait_recv()
        whole(2, q, c_s.at[2, k], c_r.at[2, k], partner).start()

    for h in (0, 1):
        for k in range(1, n_col):
            rs_copy(remote, term, rs, rs_s, rs_r, h, k, z, n_col).wait_recv()
        total = term[h, z].astype(jnp.float32)
        for k in range(1, n_col):
            total = total + rs[h, k].astype(jnp.float32)
        grad_tok[h] = total.astype(jnp.bfloat16)

    out_copy.wait()
    pltpu.make_async_copy(gp.at[p], gp_all.at[p], l_sem.at[3]).wait()
    for t in (0, 1, 2):
        for d in (0, 1):
            for s in range(n_col - 1):
                @pl.when(can_send(d, s))
                def _():
                    z_copy(t, d, s).wait_send()
        for k in range(1, n_y):
            whole(t, p, y_s.at[t, k], y_r.at[t, k], peer(2 * k)).wait_send()
        for k in range(n_y):
            q = peer(2 * k, -1)
            copy = whole(t, q, c_s.at[t, k], c_r.at[t, k], partner)
            copy.wait_send()
            if t == 2:
                copy.wait_recv()
    for m in range(1, n_dp):
        if m > 1:
            for k in range(1, n_row):
                hid_pass(m, k).wait_send()
        for h in (0, 1):
            gp_copy(h, m).wait_send()
            if m == 1:
                gp_copy(h, m).wait_recv()
            else:
                for k in range(1, n_row):
                    gp_pass(h, m, k).wait()
    for h in (0, 1):
        for m in range(n_dp):
            for k in range(1, n_row):
                x_copy(h, m, k).wait_send()
        for k in range(1, n_col):
            rs_copy(remote, term, rs, rs_s, rs_r, h, k, z, n_col).wait_send()


def rs_copy(remote, term, rs, rs_s, rs_r, h, k, z, n_col):
    to = lax.rem(z + k, n_col)
    return remote(term.at[h, to], rs.at[h, k], rs_s.at[h, k], rs_r.at[h, k], {"col": to})


def finish(factor, gp, tok, rounded, grad_in, grad_out):
    left = lax.dot_general(tok[...], gp[...], TN, preferred_element_type=jnp.float32)
    grad_in[...] = left * factor
    grad_out[...] = rounded[...].astype(jnp.float32)


def weight_gradients(factor, tile, tok, gp, rounded):
    total, width = tok.shape
    hc = gp.shape[1]
    f32 = jnp.float32
    fixed = pl.BlockSpec((total, hc), lambda i: (0, 0), pipeline_mode=pl.Buffered(1))
    moving = pl.BlockSpec((total, tile), lambda i: (0, i))
    share = hc * tile // width
    across = pl.BlockSpec((share, width), lambda i: (i, 0))
    return pl.pallas_call(
        functools.partial(finish, factor),
        grid=(width // tile,),
        out_shape=(
            jax.ShapeDtypeStruct((width, hc), f32), jax.ShapeDtypeStruct((hc, width), f32)
        ),
        in_specs=[fixed, moving, across],
        out_specs=(pl.BlockSpec((tile, hc), lambda i: (i, 0)), across),
        compiler_params=pltpu.CompilerParams(vmem_limit_bytes=60 * 1024 * 1024),
    )(gp, tok, rounded)


def shards(n_dp, n_row, n_col, tokens, cotangent, pre_act, weight_in, weight_out):
    tokc, width = tokens.shape
    rows, hidden = pre_act.shape
    hc = hidden // n_dp
    n_y = n_dp // 2
    bf, f32 = jnp.bfloat16, jnp.float32
    dma = pltpu.SemaphoreType.DMA
    anywhere = pl.BlockSpec(memory_space=pl.ANY)
    vmem = pl.BlockSpec(memory_space=pltpu.VMEM)
    total = n_dp * rows
    factor = float(total) ** (-0.5)
    half_c, half, xs = tokc // 2, rows // 2, max(n_row - 1, 1)
    tok_all, _, gp_all, _, grad_tokens, rounded = pl.pallas_call(
        functools.partial(body, n_dp, n_row, n_col, factor),
        out_shape=(
            jax.ShapeDtypeStruct((n_dp, 2, n_col, half_c, width), bf),
            jax.ShapeDtypeStruct((n_dp, 2, n_col, half_c, width), bf),
            jax.ShapeDtypeStruct((n_dp, 2, half, hc), bf),
            jax.ShapeDtypeStruct((n_dp, 2, half, hc), bf),
            jax.ShapeDtypeStruct((2, half_c, width), bf),
            jax.ShapeDtypeStruct((hc, width), bf),
        ),
        in_specs=[anywhere, anywhere, vmem, anywhere, anywhere],
        out_specs=(anywhere, anywhere, anywhere, anywhere, vmem, anywhere),
        scratch_shapes=[
            pltpu.VMEM((width, hidden), bf),
            pltpu.VMEM((max(hidden, total + hc), width), bf),
            pltpu.VMEM((n_dp, 2, half, hc), bf),
            pltpu.VMEM((n_dp, 2, half, hc), f32),
            pltpu.VMEM((n_dp, 2, half, hc), bf),
            pltpu.VMEM((xs, n_dp, 2, half, hc), bf),
            pltpu.VMEM((n_dp, 2, half, hc), bf),
            pltpu.VMEM((half, width), f32),
            pltpu.VMEM((2, n_col, half_c, width), bf),
            pltpu.VMEM((2, n_col, half_c, width), bf),
            pltpu.VMEM((2, n_col, half_c, width), bf),
            pltpu.VMEM((hc, total), bf),
            dma((2,)), dma((7,)),
            dma((2, 2, n_col)), dma((2, 2, n_col)), dma((1, 2, n_col)), dma((1, 2, n_col)),
            dma((3, n_y)), dma((3, n_y)), dma((3, n_y)), dma((3, n_y)),
            dma((n_dp,)), dma((n_dp,)), dma((n_dp, n_row)), dma((n_dp, n_row)),
            dma((2, n_dp)), dma((2, n_dp)), dma((2, n_dp, n_row)), dma((2, n_dp, n_row)),
            dma((xs, 2, n_dp)), dma((xs, 2, n_dp)),
            dma((2, n_col)), dma((2, n_col)),
        ],
        compiler_params=pltpu.CompilerParams(
            collective_id=0, has_side_effects=True, vmem_limit_bytes=62 * 1024 * 1024
        ),
    )(
        tokens.reshape(2, half_c, width), cotangent.reshape(2, half_c, width),
        pre_act, weight_in, weight_out,
    )
    grad_tokens = grad_tokens.reshape(tokc, width)
    tok_all, gp_all = tok_all.reshape(total, width), gp_all.reshape(total, hc)
    tile = width // 6 if width % (6 * 128) == 0 and hc % (6 * 16) == 0 else width // 2
    grad_in, grad_out = weight_gradients(factor, tile, tok_all, gp_all, rounded)
    return grad_tokens, grad_in, grad_out


def solution(mesh):
    in_specs = (
        P(("dp", "col"), "row"),
        P(("dp", "col"), "row"),
        P("dp", "col"),
        P("row", "col"),
        P("col", "row"),
    )
    out_specs = (P(("dp", "col"), "row"), P("row", ("col", "dp")), P(("col", "dp"), "row"))
    sizes = (mesh.shape["dp"], mesh.shape["row"], mesh.shape["col"])
    return jax.shard_map(
        functools.partial(shards, *sizes),
        mesh=mesh, in_specs=in_specs, out_specs=out_specs, check_vma=False,
    )
```
